32 devices in a mesh: sub: 8 (over z, y), grp: 4 (over x, core).
Axes of the slice: x: 2, y: 2, z: 4, core: 2. Of those that a mesh axis runs over, the one named last changes fastest.
Arguments:
- leaf_inverse: float32 [8, 4, 8, 256, 256], P('sub', 'grp'), may hold values from -0.375 to 0.375
- interior_rhs: float32 [8, 4, 8, 256, 128], P('sub', 'grp'), may hold values from -6 to 6
- interface_rhs: float32 [8, 4, 64, 128], P('sub', 'grp'), may hold values from -6 to 6
- project_basis: float32 [8, 4, 8, 4, 32, 256], P('sub', 'grp'), may hold values from -0.375 to 0.375
- lift_basis: float32 [8, 4, 8, 4, 32, 256], P('sub', 'grp'), may hold values from -0.5 to 0.5
- cluster_basis: float32 [8, 4, 32, 64], P('sub', 'grp'), may hold values from -0.1875 to 0.1875
- interface_inverse: float32 [4, 512, 512], P('grp'), may hold values from -0.25 to 0.25
- coarse_basis: float32 [4, 512, 128], P('grp'), may hold values from -0.25 to 0.25
- coarse_inverse: float32 [128, 128], replicated, may hold values from -0.25 to 0.25
- couplings: int32 [8, 4, 8, 4], P('sub', 'grp'), may hold values from 0 to 7, as said below
- ranks: int32 [8, 4, 8, 4], P('sub', 'grp'), may hold values from 8 to 32
- owners: int32 [4, 8], P('grp'), may hold values from 0 to 7, each once within a row
Outputs:
- interior: float32 [8, 4, 8, 256, 128], P('sub', 'grp')
- interface_solution: float32 [8, 4, 64, 128], P('sub', 'grp')
The draws below stay inside these ranges and needn't reach their ends.
Inputs may be any that keep to these rules, and one draw needn't show every extreme that they name: `couplings`: entries name clusters of the same group. The 4 clusters of one leaf are distinct; among one subdomain's 8 leaves no cluster is named more than 4 times, and in each group one cluster is named exactly 4 times by every subdomain of the group. Each row is a permutation: owners[g, k] is the sub index holding cluster k of group g.
All inputs are finite; a program needn't handle non-finite values.
Results may differ from the reference program's by a relative error of at most 0.000071.
Values sent between devices are 32-bit elements; how exact they have to be, the bound alone decides.
A program may use at most 128 MiB of HBM per device.

```python
import jax
import jax.numpy as jnp
from jax import lax

LS = 256
CS = 64
R = 32
P_SIZE = 128
NCO = 128
NB = 4
LV = 8
CAP = 4
NIG = 512
N_SUB = 8
N_GRP = 4


def draw_couplings(key, part):
    group_count = LV // CAP
    span = group_count * NB
    hot_groups = jax.random.randint(jax.random.fold_in(key, 11), (N_GRP,), 0, N_SUB)

    def one_group(subkey, hot_one):
        first, second = jax.random.split(subkey)
        order = jax.random.permutation(first, N_SUB)
        order = (order - order[0] + hot_one) % N_SUB
        taken = order[:span]
        offset = jax.random.randint(second, (), 0, span)
        return taken[(jnp.arange(span) + offset) % span].reshape(group_count, NB)

    def one_device(subkey, hot_one):
        group_keys = jax.random.split(subkey, CAP)
        return jax.vmap(one_group, in_axes=(0, None))(group_keys, hot_one).reshape(LV, NB)
    device_keys = jax.random.split(jax.random.fold_in(key, 5), N_SUB * N_GRP)
    hot_all = jnp.tile(hot_groups, N_SUB)
    result = jax.vmap(one_device)(device_keys, hot_all)
    return result.reshape(N_SUB, N_GRP, LV, NB).astype(jnp.int32)


def touch_ends(values, own_key, low, largest):
    dims = values.shape
    index_at = [jax.random.randint(jax.random.fold_in(own_key, axis), (), 0, dims[axis]) for axis in range(len(dims))]
    values = values.at[tuple(index_at)].set(low)
    longest = dims.index(max(dims))
    index_at[longest] = (index_at[longest] + 1) % dims[longest]
    return values.at[tuple(index_at)].set(largest)


def steps_of(rng, extent, cuts, low, high):
    def one(axis_at, blocks):
        heights = jax.random.uniform(jax.random.fold_in(jax.random.fold_in(rng, 6), axis_at), (blocks,), jnp.float32, low / len(cuts), high / len(cuts))
        return jnp.repeat(jnp.exp(heights), extent[axis_at] // blocks).reshape((-1,) + (1,) * (len(extent) - axis_at - 1))

    level = one(*cuts[0])
    for cut in cuts[1:]:
        level = level * one(*cut)
    return level


def gaussian(stream_key, dims, spread, reach, cuts=(), held_as=jnp.bfloat16):
    values = jax.random.normal(stream_key, dims, jnp.float32) * spread
    if len(cuts) > 0:
        values = steps_of(stream_key, dims, cuts, -0.22, 0.18) * values
    return jnp.clip(values, min=-reach, max=reach).astype(held_as)


def setup_inputs(seed: int = 0) -> dict:
    arg_keys = jax.random.split(jax.random.key(seed), 13)
    leaf_inverse = gaussian(arg_keys[0], (N_SUB, N_GRP, LV, LS, LS), LS ** -0.5, 0.375, ((0, 8), (1, 4)), jnp.float32)
    interior_rhs = gaussian(arg_keys[1], (N_SUB, N_GRP, LV, LS, P_SIZE), 1.0, 6.0, ((0, 8), (1, 4)), jnp.float32)
    interface_rhs = gaussian(arg_keys[2], (N_SUB, N_GRP, CS, P_SIZE), 1.0, 6.0, ((0, 8), (1, 4)), jnp.float32)
    project_basis = gaussian(arg_keys[3], (N_SUB, N_GRP, LV, NB, R, LS), LS ** -0.5, 0.375, ((0, 8), (1, 4)), jnp.float32)
    lift_basis = gaussian(arg_keys[4], (N_SUB, N_GRP, LV, NB, R, LS), (R * NB) ** -0.5, 0.5, ((0, 8), (1, 4)), jnp.float32)
    cluster_basis = gaussian(arg_keys[5], (N_SUB, N_GRP, R, CS), (R * LV * NB) ** -0.5, 0.1875, ((0, 8), (1, 4)), jnp.float32)
    interface_inverse = gaussian(arg_keys[6], (N_GRP, NIG, NIG), NIG ** -0.5, 0.25, ((0, 4),), jnp.float32)
    coarse_basis = gaussian(arg_keys[7], (N_GRP, NIG, NCO), NIG ** -0.5, 0.25, ((0, 4),), jnp.float32)
    coarse_inverse = gaussian(arg_keys[8], (NCO, NCO), (NCO * N_GRP) ** -0.5, 0.25, (), jnp.float32)
    couplings = draw_couplings(jax.random.fold_in(arg_keys[12], 71), 0)
    ranks = touch_ends(jax.random.randint(arg_keys[10], (N_SUB, N_GRP, LV, NB), R // 4, R + 1), jax.random.fold_in(arg_keys[10], 1), R // 4, R).astype(jnp.int32)
    owners = jax.vmap(lambda own: jax.random.permutation(own, N_SUB))(jax.random.split(arg_keys[11], N_GRP)).reshape((N_GRP, N_SUB)).astype(jnp.int32)
    return dict(leaf_inverse=leaf_inverse, interior_rhs=interior_rhs, interface_rhs=interface_rhs, project_basis=project_basis, lift_basis=lift_basis, cluster_basis=cluster_basis, interface_inverse=interface_inverse, coarse_basis=coarse_basis, coarse_inverse=coarse_inverse, couplings=couplings, ranks=ranks, owners=owners)


highest = lax.Precision.HIGHEST


def reference(leaf_inverse, interior_rhs, interface_rhs, project_basis, lift_basis, cluster_basis, interface_inverse, coarse_basis, coarse_inverse, couplings, ranks, owners):
    solved = jnp.einsum('sglij,sgljp->sglip', leaf_inverse, interior_rhs, precision=highest)
    rank_mask = (jnp.arange(R, dtype=jnp.int32)[None, None, None, None, :] < ranks[..., None]).astype(jnp.float32)
    coefficients = jnp.einsum('sgljri,sglip->sgljrp', project_basis, solved, precision=highest) * rank_mask[..., None]
    cluster_pick = (couplings[..., None] == jnp.arange(N_SUB, dtype=jnp.int32)).astype(jnp.float32)
    summed = jnp.einsum('sgljk,sgljrp->gkrp', cluster_pick, coefficients, precision=highest)
    owner_pick = (owners[:, :, None] == jnp.arange(N_SUB, dtype=jnp.int32)[None, None, :]).astype(jnp.float32)
    by_owner = jnp.einsum('gkt,gkrp->tgrp', owner_pick, summed, precision=highest)
    interface_terms = interface_rhs - jnp.einsum('sgrc,sgrp->sgcp', cluster_basis, by_owner, precision=highest)
    by_cluster = jnp.einsum('gks,sgcp->gkcp', owner_pick, interface_terms, precision=highest).reshape(N_GRP, NIG, P_SIZE)
    local_part = jnp.einsum('gij,gjp->gip', interface_inverse, by_cluster, precision=highest)
    coarse_residual = jnp.einsum('gin,gip->np', coarse_basis, by_cluster, precision=highest)
    coarse_solution = jnp.dot(coarse_inverse, coarse_residual, precision=highest)
    solution = local_part + jnp.einsum('gin,np->gip', coarse_basis, coarse_solution, precision=highest)
    solution_owner = jnp.einsum('gks,gkcp->sgcp', owner_pick, solution.reshape(N_GRP, N_SUB, CS, P_SIZE), precision=highest)
    lifted = jnp.einsum('sgrc,sgcp->sgrp', cluster_basis, solution_owner, precision=highest)
    lifted_cluster = jnp.einsum('gks,sgrp->gkrp', owner_pick, lifted, precision=highest)
    returned = jnp.einsum('sgljk,gkrp->sgljrp', cluster_pick, lifted_cluster, precision=highest) * rank_mask[..., None]
    correction = jnp.einsum('sgljri,sgljrp->sglip', lift_basis, returned, precision=highest)
    interior = solved - jnp.einsum('sglij,sgljp->sglip', leaf_inverse, correction, precision=highest)
    return interior, solution_owner
```

```python
import functools

import jax
import jax.numpy as jnp
from jax import lax
from jax.experimental import pallas as pl
from jax.experimental.pallas import tpu as pltpu
from jax.sharding import PartitionSpec as P

highest = lax.Precision.HIGHEST
MESH = pl.DeviceIdType.MESH
F32 = jnp.float32
BF16 = jnp.bfloat16


def split(x):
    high = x.astype(BF16)
    return high, (x - high.astype(F32)).astype(BF16)


def dot(a, b, dims=((1,), (0,))):
    return lax.dot_general(a, b, (dims, ((), ())), preferred_element_type=F32)


def product(a, b, dims=((1,), (0,))):
    return dot(a[0], b[0], dims) + dot(a[0], b[1], dims) + dot(a[1], b[0], dims)


def narrow(a, b):
    width = b[0].shape[1]
    both = dot(a[0], jnp.concatenate([b[0], b[1]], axis=1))
    return both[:, :width] + both[:, width:] + dot(a[1], b[0])


def kernel(
    n,
    groups,
    linv_hbm,
    rhs_hbm,
    irhs_hbm,
    proj_hbm,
    lift_hbm,
    basis_hbm,
    inverse_hbm,
    coarse_hbm,
    cinv_hbm,
    couplings,
    ranks,
    owners,
    interior_hbm,
    own_out,
    linv,
    rhs,
    proj,
    lift,
    inverse,
    coarse,
    cinv,
    g_basis,
    g_irhs,
    sums,
    coarse_out,
    in_sums,
    in_coarse,
    mid,
    in_mid,
    g_sums,
    g_coarse,
    bct,
    gain,
    base,
    solved,
    back,
    lifted,
    result,
    leaf_sem,
    misc_sem,
    out_sem,
    pre_send,
    pre_recv,
    a_send,
    a_recv,
    m_send,
    m_recv,
    b_send,
    b_recv,
):
    leaves, ls, ports = rhs.shape
    blocks = couplings.shape[1]
    rank = g_basis.shape[1]
    cs = g_basis.shape[2]
    nco = coarse.shape[2]
    piece = nco // n
    me = lax.axis_index("sub")
    my_group = lax.axis_index("grp")

    def leaf_copy(l, which):
        pair = ((linv_hbm, linv), (rhs_hbm, rhs), (proj_hbm, proj), (lift_hbm, lift))[which]
        return pltpu.make_async_copy(pair[0].at[l], pair[1].at[l], leaf_sem.at[which, l])

    barrier = pltpu.get_barrier_semaphore()
    for d in range(1, n):
        pl.semaphore_signal(barrier, inc=1, device_id=(lax.rem(me + d, n), my_group), device_id_type=MESH)
    for d in range(1, groups):
        pl.semaphore_signal(barrier, inc=1, device_id=(me, lax.rem(my_group + d, groups)), device_id_type=MESH)
    for l in range(leaves):
        for which in range(3):
            leaf_copy(l, which).start()
    misc = (
        pltpu.make_async_copy(basis_hbm, g_basis.at[me], misc_sem.at[0]),
        pltpu.make_async_copy(irhs_hbm, g_irhs.at[me], misc_sem.at[1]),
        pltpu.make_async_copy(coarse_hbm, coarse, misc_sem.at[2]),
        pltpu.make_async_copy(inverse_hbm, inverse, misc_sem.at[3]),
        pltpu.make_async_copy(cinv_hbm, cinv, misc_sem.at[4]),
    )
    for copy in misc:
        copy.start()
    for l in range(leaves):
        leaf_copy(l, 3).start()

    sums[...] = jnp.zeros_like(sums)
    row_of = lax.broadcasted_iota(jnp.int32, (rank, ports), 0)

    def leaf_forward(l):
        for which in range(3):
            leaf_copy(l, which).wait()
        both = product(split(proj[l]), split(linv[l]))
        coef = narrow(split(both), split(rhs[l]))
        for j in range(blocks):
            kept = jnp.where(row_of < ranks[l, j], coef[j * rank : (j + 1) * rank], 0.0)
            for k in range(n):
                sums[k] += jnp.where(couplings[l, j] == k, kept, 0.0)

    leaf_forward(0)

    pl.semaphore_wait(barrier, n - 1 + groups - 1)

    def peer(d):
        return (lax.rem(me + d, n), my_group)

    def source(d):
        return lax.rem(me - d + n, n)

    def pre_copy(d, which, slot):
        src, dst = ((basis_hbm, g_basis), (irhs_hbm, g_irhs))[which]
        return pltpu.make_async_remote_copy(
            src_ref=src, dst_ref=dst.at[slot], send_sem=pre_send.at[which, d], recv_sem=pre_recv.at[which, d],
            device_id=peer(d), device_id_type=MESH,
        )

    for which in range(2):
        for d in range(1, n):
            pre_copy(d, which, me).start()

    pl.loop(1, leaves)(leaf_forward)

    def sums_copy(d):
        return pltpu.make_async_remote_copy(
            src_ref=sums.at[lax.rem(me + d, n)], dst_ref=in_sums.at[d], send_sem=a_send.at[0, d],
            recv_sem=a_recv.at[0, d], device_id=peer(d), device_id_type=MESH,
        )

    def coarse_copy(d):
        return pltpu.make_async_remote_copy(
            src_ref=coarse_out.at[lax.rem(me + d, n)], dst_ref=in_coarse.at[d], send_sem=a_send.at[1, d],
            recv_sem=a_recv.at[1, d], device_id=peer(d), device_id_type=MESH,
        )

    for d in range(1, n):
        sums_copy(d).start()

    for copy in misc:
        copy.wait()
    for which in range(2):
        for d in range(1, n):
            pre_copy(d, which, source(d)).wait_recv()

    stacked = jnp.concatenate([g_basis[owners[0, k]] for k in range(n)], axis=0)
    wide = jnp.concatenate([stacked] * n, axis=1)
    diag_row = lax.broadcasted_iota(jnp.int32, wide.shape, 0) // rank
    diag_col = lax.broadcasted_iota(jnp.int32, wide.shape, 1) // cs
    diagonal = split(jnp.where(diag_row == diag_col, wide, 0.0))
    own = jnp.int32(0)
    for k in range(n):
        own = jnp.where(owners[0, k] == me, k, own)
    coarse_pair = split(coarse[...].reshape(n * cs, nco))
    basis_coarse = narrow(diagonal, coarse_pair)
    own_coarse = coarse[own]
    bct[...] = basis_coarse.T
    sums_pair = split(sums[...].reshape(n * rank, ports))
    part = narrow(split(own_coarse.T), split(g_irhs[me])) - narrow(split(bct[...]), sums_pair)
    coarse_out[...] = part.reshape(n, piece, ports)
    for d in range(1, n):
        coarse_copy(d).start()

    own_rows = inverse[own]
    inverse_pair = split(inverse[...].reshape(n * cs, n * cs))
    left = jnp.concatenate([product(diagonal, inverse_pair), own_rows], axis=0)
    left_pair = split(left)
    irhs_all = jnp.concatenate([g_irhs[owners[0, k]] for k in range(n)], axis=0)
    base[...] = narrow(left_pair, split(irhs_all))
    gain[:, : n * rank] = -product(left_pair, diagonal, ((1,), (1,)))
    coarse_left = jnp.concatenate([basis_coarse, own_coarse], axis=0)
    gain[:, n * rank :] = narrow(split(coarse_left), split(cinv[...]))

    def gather_copy(d, which, slot):
        ref = (g_sums, g_coarse)[which]
        return pltpu.make_async_remote_copy(
            src_ref=ref.at[me], dst_ref=ref.at[slot], send_sem=b_send.at[which, d], recv_sem=b_recv.at[which, d],
            device_id=peer(d), device_id_type=MESH,
        )

    total = sums[me]
    for d in range(1, n):
        sums_copy(d).wait_recv()
        total = total + in_sums[d]
    g_sums[me] = total
    for d in range(1, n):
        gather_copy(d, 0, me).start()

    def mid_copy(d):
        return pltpu.make_async_remote_copy(
            src_ref=mid, dst_ref=in_mid.at[d], send_sem=m_send.at[d], recv_sem=m_recv.at[d],
            device_id=(me, lax.rem(my_group + d, groups)), device_id_type=MESH,
        )

    coarse_total = coarse_out[me]
    for d in range(1, n):
        coarse_copy(d).wait_recv()
        coarse_total = coarse_total + in_coarse[d]
    mid[...] = coarse_total
    for d in range(1, groups):
        mid_copy(d).start()

    def leaf_middle(l):
        leaf_copy(l, 3).wait()
        inv = split(linv[l])
        solved[l] = narrow(inv, split(rhs[l]))
        spread = product(inv, split(lift[l]), ((1,), (1,)))
        back[l] = jnp.concatenate(split(spread), axis=1)

    half = leaves // 4
    pl.loop(0, half)(leaf_middle)

    for d in range(1, groups):
        mid_copy(d).wait_recv()
        coarse_total = coarse_total + in_mid[d]
    g_coarse[me] = coarse_total
    for d in range(1, n):
        gather_copy(d, 1, me).start()

    pl.loop(half, leaves)(leaf_middle)

    for which in range(2):
        for d in range(1, n):
            gather_copy(d, which, source(d)).wait_recv()

    known = jnp.concatenate([g_sums[...].reshape(n * rank, ports), g_coarse[...].reshape(nco, ports)], axis=0)
    final = base[...] + narrow(split(gain[...]), split(known))
    lifted[...] = final[: n * rank].reshape(n, rank, ports)
    own_out[...] = final[n * rank :]

    def out_copy(l):
        return pltpu.make_async_copy(result.at[l], interior_hbm.at[l], out_sem.at[l])

    @pl.loop(0, leaves)
    def leaf_back(l):
        rows = []
        for j in range(blocks):
            rows.append(jnp.where(row_of < ranks[l, j], lifted[couplings[l, j]], 0.0))
        pair = jnp.concatenate(split(jnp.concatenate(rows, axis=0)), axis=1)
        both = dot(back[l], jnp.concatenate([pair, pair], axis=0))
        result[l] = solved[l] - (both[:, :ports] + both[:, ports:])
        out_copy(l).start()

    for l in range(leaves):
        out_copy(l).wait()
    for d in range(1, n):
        for which in range(2):
            pre_copy(d, which, me).wait_send()
            gather_copy(d, which, me).wait_send()
        sums_copy(d).wait_send()
        coarse_copy(d).wait_send()
    for d in range(1, groups):
        mid_copy(d).wait_send()


def fused(
    leaf_inverse,
    interior_rhs,
    interface_rhs,
    project_basis,
    lift_basis,
    cluster_basis,
    interface_inverse,
    coarse_basis,
    coarse_inverse,
    couplings,
    ranks,
    owners,
):
    n = lax.axis_size("sub")
    groups = lax.axis_size("grp")
    leaves, ls = leaf_inverse.shape[2:4]
    ports = interior_rhs.shape[4]
    blocks, rank = project_basis.shape[3:5]
    cs = cluster_basis.shape[3]
    nig = interface_inverse.shape[1]
    nco = coarse_basis.shape[2]
    piece = nco // n
    hbm = pl.BlockSpec(memory_space=pl.ANY)
    smem = pl.BlockSpec(memory_space=pltpu.SMEM)
    dma = pltpu.SemaphoreType.DMA
    interior, own = pl.pallas_call(
        functools.partial(kernel, n, groups),
        out_shape=(
            jax.ShapeDtypeStruct((leaves, ls, ports), F32),
            jax.ShapeDtypeStruct((cs, ports), F32),
        ),
        in_specs=[hbm] * 9 + [smem] * 3,
        out_specs=(hbm, pl.BlockSpec(memory_space=pltpu.VMEM)),
        scratch_shapes=[
            pltpu.VMEM((leaves, ls, ls), F32),
            pltpu.VMEM((leaves, ls, ports), F32),
            pltpu.VMEM((leaves, blocks * rank, ls), F32),
            pltpu.VMEM((leaves, blocks * rank, ls), F32),
            pltpu.VMEM((n, cs, nig), F32),
            pltpu.VMEM((n, cs, nco), F32),
            pltpu.VMEM((nco, nco), F32),
            pltpu.VMEM((n, rank, cs), F32),
            pltpu.VMEM((n, cs, ports), F32),
            pltpu.VMEM((n, rank, ports), F32),
            pltpu.VMEM((n, piece, ports), F32),
            pltpu.VMEM((n, rank, ports), F32),
            pltpu.VMEM((n, piece, ports), F32),
            pltpu.VMEM((piece, ports), F32),
            pltpu.VMEM((groups, piece, ports), F32),
            pltpu.VMEM((n, rank, ports), F32),
            pltpu.VMEM((n, piece, ports), F32),
            pltpu.VMEM((nco, n * rank), F32),
            pltpu.VMEM((n * rank + cs, n * rank + nco), F32),
            pltpu.VMEM((n * rank + cs, ports), F32),
            pltpu.VMEM((leaves, ls, ports), F32),
            pltpu.VMEM((leaves, ls, 2 * blocks * rank), BF16),
            pltpu.VMEM((n, rank, ports), F32),
            pltpu.VMEM((leaves, ls, ports), F32),
            dma((4, leaves)),
            dma((5,)),
            dma((leaves,)),
            dma((2, n)),
            dma((2, n)),
            dma((2, n)),
            dma((2, n)),
            dma((groups,)),
            dma((groups,)),
            dma((2, n)),
            dma((2, n)),
        ],
        compiler_params=pltpu.CompilerParams(
            collective_id=0, has_side_effects=True, vmem_limit_bytes=48 * 1024 * 1024
        ),
    )(
        leaf_inverse[0, 0],
        interior_rhs[0, 0],
        interface_rhs[0, 0],
        project_basis.reshape(leaves, blocks * rank, ls),
        lift_basis.reshape(leaves, blocks * rank, ls),
        cluster_basis[0, 0],
        interface_inverse.reshape(n, cs, nig),
        coarse_basis.reshape(n, cs, nco),
        coarse_inverse,
        couplings[0, 0],
        ranks[0, 0],
        owners,
    )
    return interior[None, None], own[None, None]


def shards(
    leaf_inverse,
    interior_rhs,
    interface_rhs,
    project_basis,
    lift_basis,
    cluster_basis,
    interface_inverse,
    coarse_basis,
    coarse_inverse,
    couplings,
    ranks,
    owners,
):
    linv_local = leaf_inverse[0, 0]
    leaves = couplings.shape[2]
    blocks = couplings.shape[3]
    rank_pad = project_basis.shape[4]
    port_count = interior_rhs.shape[4]
    cluster_width = cluster_basis.shape[3]
    sub_count = lax.axis_size("sub")
    block_count = leaves * blocks
    solved = jnp.einsum("lij,ljp->lip", linv_local, interior_rhs[0, 0], precision=highest)
    rank_mask = (
        jnp.arange(rank_pad, dtype=jnp.int32)[None, None, :] < ranks[0, 0][..., None]
    ).astype(jnp.float32)
    coefficients = (
        jnp.einsum("ljri,lip->ljrp", project_basis[0, 0], solved, precision=highest)
        * rank_mask[..., None]
    )
    flat_coef = coefficients.reshape(block_count, rank_pad, port_count)
    owner_table = owners[0]
    sub_range = jnp.arange(sub_count, dtype=jnp.int32)
    cluster_hot = (couplings[0, 0].reshape(block_count)[:, None] == sub_range[None, :]).astype(
        jnp.int32
    )
    target = jnp.sum(cluster_hot * owner_table[None, :], axis=1)
    owner_matrix = (owner_table[:, None] == sub_range[None, :]).astype(jnp.float32)
    capacity = max(2, block_count // sub_count)
    block_range = jnp.arange(block_count, dtype=jnp.int32)
    earlier = (target[:, None] == target[None, :]) & (block_range[None, :] < block_range[:, None])
    slot_index = jnp.sum(earlier.astype(jnp.int32), axis=1)
    slot_place = target * capacity + slot_index
    dispatch = (
        slot_place[:, None] == jnp.arange(sub_count * capacity, dtype=jnp.int32)[None, :]
    ).astype(jnp.float32)
    outgoing = jnp.einsum("mq,mrp->qrp", dispatch, flat_coef, precision=highest).reshape(
        sub_count, capacity, rank_pad, port_count
    )
    filled = jnp.sum(dispatch, axis=0).reshape(sub_count, capacity)
    incoming, filled_in = (
        lax.all_to_all(outgoing, "sub", split_axis=0, concat_axis=0, tiled=True),
        lax.all_to_all(filled, "sub", split_axis=0, concat_axis=0, tiled=True),
    )
    gathered_coef = jnp.sum(incoming, axis=(0, 1))
    own_basis = cluster_basis[0, 0]
    interface_terms = interface_rhs[0, 0] - lax.dot_general(
        own_basis, gathered_coef, (((0,), (0,)), ((), ())), precision=highest
    )
    port_share = port_count // sub_count
    by_share = interface_terms.T.reshape(sub_count, port_share * cluster_width)
    spread = lax.all_to_all(by_share, "sub", split_axis=0, concat_axis=0, tiled=True).reshape(
        sub_count, port_share, cluster_width
    )
    ordered = jnp.einsum("ks,spc->pkc", owner_matrix, spread, precision=highest).reshape(
        port_share, sub_count * cluster_width
    )
    local_part = lax.dot_general(
        ordered, interface_inverse[0], (((1,), (1,)), ((), ())), precision=highest
    )
    coarse_local = jnp.dot(ordered, coarse_basis[0], precision=highest)
    coarse_residual = lax.psum(coarse_local, "grp")
    coarse_solution = lax.dot_general(
        coarse_residual, coarse_inverse, (((1,), (1,)), ((), ())), precision=highest
    )
    solution = local_part + lax.dot_general(
        coarse_solution, coarse_basis[0], (((1,), (1,)), ((), ())), precision=highest
    )
    owner_order = jnp.einsum(
        "ks,pkc->spc",
        owner_matrix,
        solution.reshape(port_share, sub_count, cluster_width),
        precision=highest,
    )
    back_rows = lax.all_to_all(
        owner_order.reshape(sub_count, port_share * cluster_width),
        "sub",
        split_axis=0,
        concat_axis=0,
        tiled=True,
    )
    own_solution = back_rows.reshape(port_count, cluster_width).T
    lifted = jnp.dot(own_basis, own_solution, precision=highest)
    replies = filled_in[:, :, None, None] * lifted[None, None]
    returned = lax.all_to_all(replies, "sub", split_axis=0, concat_axis=0, tiled=True).reshape(
        -1, rank_pad, port_count
    )
    per_block = jnp.einsum("mq,qrp->mrp", dispatch, returned, precision=highest)
    per_block = per_block.reshape(leaves, blocks, rank_pad, port_count) * rank_mask[..., None]
    correction = jnp.einsum("ljri,ljrp->lip", lift_basis[0, 0], per_block, precision=highest)
    interior = solved - jnp.einsum("lij,ljp->lip", linv_local, correction, precision=highest)
    return (interior[None, None], own_solution[None, None])


def solution(mesh):
    in_specs = (
        P("sub", "grp", None, None, None),
        P("sub", "grp", None, None, None),
        P("sub", "grp", None, None),
        P("sub", "grp", None, None, None, None),
        P("sub", "grp", None, None, None, None),
        P("sub", "grp", None, None),
        P("grp", None, None),
        P("grp", None, None),
        P(),
        P("sub", "grp", None, None),
        P("sub", "grp", None, None),
        P("grp", None),
    )
    out_specs = (P("sub", "grp", None, None, None), P("sub", "grp", None, None))
    body = fused if mesh.shape["sub"] <= 8 else shards
    return jax.shard_map(body, mesh=mesh, in_specs=in_specs, out_specs=out_specs, check_vma=False)
```

```python
import functools

import jax
import jax.numpy as jnp
from jax import lax
from jax.experimental import pallas as pl
from jax.experimental.pallas import tpu as pltpu
from jax.sharding import PartitionSpec as P

highest = lax.Precision.HIGHEST
MESH = pl.DeviceIdType.MESH
F32 = jnp.float32
BF16 = jnp.bfloat16


def split(x):
    high = x.astype(BF16)
    return high, (x - high.astype(F32)).astype(BF16)


def dot(a, b, dims=((1,), (0,))):
    return lax.dot_general(a, b, (dims, ((), ())), preferred_element_type=F32)


def product(a, b, dims=((1,), (0,))):
    return dot(a[0], b[0], dims) + dot(a[0], b[1], dims) + dot(a[1], b[0], dims)


def narrow(a, b):
    width = b[0].shape[1]
    both = dot(a[0], jnp.concatenate([b[0], b[1]], axis=1))
    return both[:, :width] + both[:, width:] + dot(a[1], b[0])


def kernel(
    n,
    groups,
    linv_hbm,
    rhs_hbm,
    irhs_hbm,
    proj_hbm,
    lift_hbm,
    basis_hbm,
    inverse_hbm,
    coarse_hbm,
    cinv_hbm,
    couplings,
    ranks,
    owners,
    solved,
    back,
    lifted,
    own_out,
    linv,
    rhs,
    proj,
    lift,
    inverse,
    coarse,
    cinv,
    basis_own,
    irhs_own,
    pre_out,
    pre_in,
    sums,
    a_out,
    a_in,
    mid,
    mid_in,
    share,
    lift_all,
    sol,
    own_stage,
    own_in,
    gain,
    base,
    leaf_sem,
    misc_sem,
    pre_send,
    pre_recv,
    a_send,
    a_recv,
    m_send,
    m_recv,
    b_send,
    b_recv,
    o_send,
    o_recv,
):
    leaves, ls, ports = rhs.shape
    blocks = couplings.shape[2]
    rank, cs = basis_own.shape
    nco = coarse.shape[1]
    part = ports // n
    half_rank, half_part = rank // 2, part // 2
    me = lax.axis_index("sub")
    my_group = lax.axis_index("grp")

    def leaf_copy(l, which):
        pair = ((linv_hbm, linv), (rhs_hbm, rhs), (proj_hbm, proj), (lift_hbm, lift))[which]
        return pltpu.make_async_copy(pair[0].at[l], pair[1].at[l], leaf_sem.at[which, l])

    barrier = pltpu.get_barrier_semaphore()
    for d in range(1, n):
        pl.semaphore_signal(barrier, inc=1, device_id=(lax.rem(me + d, n), my_group), device_id_type=MESH)
    for d in range(1, groups):
        pl.semaphore_signal(barrier, inc=1, device_id=(me, lax.rem(my_group + d, groups)), device_id_type=MESH)
    for l in range(leaves):
        for which in range(3):
            leaf_copy(l, which).start()
    misc = (
        pltpu.make_async_copy(basis_hbm, basis_own, misc_sem.at[0]),
        pltpu.make_async_copy(irhs_hbm, irhs_own, misc_sem.at[1]),
        pltpu.make_async_copy(coarse_hbm, coarse, misc_sem.at[2]),
        pltpu.make_async_copy(inverse_hbm, inverse, misc_sem.at[3]),
        pltpu.make_async_copy(cinv_hbm, cinv, misc_sem.at[4]),
    )
    for copy in misc:
        copy.start()
    for l in range(leaves):
        leaf_copy(l, 3).start()

    sums[...] = jnp.zeros_like(sums)
    row_of = lax.broadcasted_iota(jnp.int32, (rank, ports), 0)

    def leaf_forward(l):
        for which in range(3):
            leaf_copy(l, which).wait()
        both = product(split(proj[l]), split(linv[l]))
        coef = narrow(split(both), split(rhs[l]))
        for j in range(blocks):
            kept = jnp.where(row_of < ranks[0, 0, j, l], coef[j * rank : (j + 1) * rank], 0.0)
            for k in range(n):
                sums[k] += jnp.where(couplings[0, 0, j, l] == k, kept, 0.0)

    misc[0].wait()
    misc[1].wait()
    packed = jnp.concatenate([basis_own[:half_rank], basis_own[half_rank:]], axis=1)
    irhs_t = irhs_own[...].T
    for t in range(n):
        pre_out[t, :half_rank] = packed
        rows = irhs_t[t * part : (t + 1) * part]
        pre_out[t, half_rank:] = jnp.concatenate([rows[:half_part], rows[half_part:]], axis=1)

    def peer(d):
        return (lax.rem(me + d, n), my_group)

    def source(d):
        return lax.rem(me - d + n, n)

    def remote(src, dst, send, recv, target):
        return pltpu.make_async_remote_copy(
            src_ref=src, dst_ref=dst, send_sem=send, recv_sem=recv, device_id=target, device_id_type=MESH
        )

    def pre_copy(d, slot):
        return remote(pre_out.at[lax.rem(me + d, n)], pre_in.at[slot], pre_send.at[d], pre_recv.at[d], peer(d))

    def sums_copy(d):
        return remote(a_out.at[lax.rem(me + d, n)], a_in.at[d], a_send.at[d], a_recv.at[d], peer(d))

    def mid_copy(d):
        target = (me, lax.rem(my_group + d, groups))
        return remote(mid, mid_in.at[d], m_send.at[d], m_recv.at[d], target)

    def gather_copy(d, slot):
        return remote(share, lift_all.at[slot], b_send.at[d], b_recv.at[d], peer(d))

    def own_copy(d, slot):
        return remote(own_stage.at[lax.rem(me + d, n)], own_in.at[slot], o_send.at[d], o_recv.at[d], peer(d))

    pl.semaphore_wait(barrier, n - 1 + groups - 1)
    for d in range(1, n):
        pre_copy(d, me).start()
    pre_in[me] = pre_out[me]

    pl.loop(0, leaves)(leaf_forward)

    sums_t = sums[...].reshape(n * rank, ports).T
    a_out[...] = sums_t.reshape(n, part, n * rank)
    for d in range(1, n):
        sums_copy(d).start()

    for copy in misc[2:]:
        copy.wait()
    for d in range(1, n):
        pre_copy(d, source(d)).wait_recv()
    got = [pre_in[owners[0, k]] for k in range(n)]
    stacked = jnp.concatenate(
        [half for g in got for half in (g[:half_rank, :cs], g[:half_rank, cs:])], axis=0
    )
    wide = jnp.concatenate([stacked] * n, axis=1)
    diag_row = lax.broadcasted_iota(jnp.int32, wide.shape, 0) // rank
    diag_col = lax.broadcasted_iota(jnp.int32, wide.shape, 1) // cs
    diagonal = split(jnp.where(diag_row == diag_col, wide, 0.0))
    irhs_share = jnp.concatenate(
        [jnp.concatenate([g[half_rank:, :cs], g[half_rank:, cs:]], axis=0) for g in got], axis=1
    )
    irhs_pair = split(irhs_share)
    coarse_pair = split(coarse[...])
    inverse_pair = split(inverse[...])
    basis_coarse = narrow(diagonal, coarse_pair)
    basis_coarse_pair = split(basis_coarse)
    left_pair = split(product(diagonal, inverse_pair))
    base[...] = product(irhs_pair, left_pair, ((1,), (1,)))
    gain[:, : n * rank] = -product(left_pair, diagonal, ((1,), (1,)))
    gain[:, n * rank :] = narrow(basis_coarse_pair, split(cinv[...]))
    coarse_base = narrow(irhs_pair, coarse_pair)

    total = a_out[me]
    for d in range(1, n):
        sums_copy(d).wait_recv()
        total = total + a_in[d]
    total_pair = split(total)
    residual = coarse_base - narrow(total_pair, basis_coarse_pair)
    mid[...] = residual
    for d in range(1, groups):
        mid_copy(d).start()

    def leaf_middle(l):
        leaf_copy(l, 3).wait()
        inv = split(linv[l])
        solved[l] = narrow(inv, split(rhs[l]))
        spread = product(inv, split(lift[l]), ((1,), (1,)))
        back[l] = jnp.concatenate(split(spread), axis=1)

    half = leaves // 4
    pl.loop(0, half)(leaf_middle)

    for d in range(1, groups):
        mid_copy(d).wait_recv()
        residual = residual + mid_in[d]
    known = jnp.concatenate([total, residual], axis=1)
    share[...] = base[...] + product(split(known), split(gain[...]), ((1,), (1,)))
    for d in range(1, n):
        gather_copy(d, me).start()
    lift_all[me] = share[...]

    by_cluster = split(irhs_share - product(total_pair, diagonal))
    coarse_solution = split(product(split(residual), split(cinv[...]), ((1,), (1,))))
    solution_t = product(by_cluster, inverse_pair, ((1,), (1,))) + product(coarse_solution, coarse_pair, ((1,), (1,)))
    for k in range(n):
        rows = solution_t[:, k * cs : (k + 1) * cs]
        sol[k] = jnp.concatenate([rows[:half_part], rows[half_part:]], axis=1)
    for t in range(n):
        place = jnp.int32(0)
        for k in range(n):
            place = jnp.where(owners[0, k] == t, k, place)
        own_stage[t] = sol[place]
    for d in range(1, n):
        own_copy(d, me).start()
    own_in[me] = own_stage[me]

    pl.loop(half, leaves)(leaf_middle)

    for d in range(1, n):
        gather_copy(d, source(d)).wait_recv()
    lifted[...] = lift_all[...].reshape(ports, n * rank).T.reshape(n, rank, ports)
    for d in range(1, n):
        own_copy(d, source(d)).wait_recv()
    rows = []
    for t in range(n):
        rows += [own_in[t][:, :cs], own_in[t][:, cs:]]
    own_out[...] = jnp.concatenate(rows, axis=0).T

    for d in range(1, n):
        pre_copy(d, me).wait_send()
        sums_copy(d).wait_send()
        gather_copy(d, me).wait_send()
        own_copy(d, me).wait_send()
    for d in range(1, groups):
        mid_copy(d).wait_send()


def finish(solved, back, lifted, own, couplings, ranks, interior_hbm, own_hbm, result, out_sem, own_sem):
    leaves, ls, ports = solved.shape
    blocks = couplings.shape[2]
    rank = lifted.shape[1]
    row_of = lax.broadcasted_iota(jnp.int32, (rank, ports), 0)
    own_copy = pltpu.make_async_copy(own, own_hbm, own_sem)
    own_copy.start()

    def out_copy(l):
        return pltpu.make_async_copy(result.at[l], interior_hbm.at[l], out_sem.at[l])

    for l in range(leaves):
        rows = []
        for j in range(blocks):
            rows.append(jnp.where(row_of < ranks[0, 0, j, l], lifted[couplings[0, 0, j, l]], 0.0))
        pair = jnp.concatenate(split(jnp.concatenate(rows, axis=0)), axis=1)
        both = dot(back[l], jnp.concatenate([pair, pair], axis=0))
        result[l] = solved[l] - (both[:, :ports] + both[:, ports:])
        out_copy(l).start()
    for l in range(leaves):
        out_copy(l).wait()
    own_copy.wait()


def fused(
    leaf_inverse,
    interior_rhs,
    interface_rhs,
    project_basis,
    lift_basis,
    cluster_basis,
    interface_inverse,
    coarse_basis,
    coarse_inverse,
    couplings,
    ranks,
    owners,
):
    n = lax.axis_size("sub")
    groups = lax.axis_size("grp")
    leaves, ls = leaf_inverse.shape[2:4]
    ports = interior_rhs.shape[4]
    blocks, rank = project_basis.shape[3:5]
    cs = cluster_basis.shape[3]
    nig = interface_inverse.shape[1]
    nco = coarse_basis.shape[2]
    part = ports // n
    hbm = pl.BlockSpec(memory_space=pltpu.HBM)
    smem = pl.BlockSpec(memory_space=pltpu.SMEM)
    vmem = pl.BlockSpec(memory_space=pltpu.VMEM)
    dma = pltpu.SemaphoreType.DMA
    couplings = jnp.swapaxes(couplings, 2, 3)
    ranks = jnp.swapaxes(ranks, 2, 3)
    held = pl.pallas_call(
        functools.partial(kernel, n, groups),
        out_shape=(
            pltpu.VMEM((leaves, ls, ports), F32),
            pltpu.VMEM((leaves, ls, 2 * blocks * rank), BF16),
            pltpu.VMEM((n, rank, ports), F32),
            pltpu.VMEM((cs, ports), F32),
        ),
        in_specs=[hbm] * 9 + [smem] * 3,
        out_specs=(vmem,) * 4,
        scratch_shapes=[
            pltpu.VMEM((leaves, ls, ls), F32),
            pltpu.VMEM((leaves, ls, ports), F32),
            pltpu.VMEM((leaves, blocks * rank, ls), F32),
            pltpu.VMEM((leaves, blocks * rank, ls), F32),
            pltpu.VMEM((nig, nig), F32),
            pltpu.VMEM((nig, nco), F32),
            pltpu.VMEM((nco, nco), F32),
            pltpu.VMEM((rank, cs), F32),
            pltpu.VMEM((cs, ports), F32),
            pltpu.VMEM((n, rank // 2 + part // 2, 2 * cs), F32),
            pltpu.VMEM((n, rank // 2 + part // 2, 2 * cs), F32),
            pltpu.VMEM((n, rank, ports), F32),
            pltpu.VMEM((n, part, n * rank), F32),
            pltpu.VMEM((n, part, n * rank), F32),
            pltpu.VMEM((part, nco), F32),
            pltpu.VMEM((groups, part, nco), F32),
            pltpu.VMEM((part, n * rank), F32),
            pltpu.VMEM((n, part, n * rank), F32),
            pltpu.VMEM((n, part // 2, 2 * cs), F32),
            pltpu.VMEM((n, part // 2, 2 * cs), F32),
            pltpu.VMEM((n, part // 2, 2 * cs), F32),
            pltpu.VMEM((n * rank, n * rank + nco), F32),
            pltpu.VMEM((part, n * rank), F32),
            dma((4, leaves)),
            dma((5,)),
        ]
        + [dma((n,))] * 4
        + [dma((groups,))] * 2
        + [dma((n,))] * 4,
        compiler_params=pltpu.CompilerParams(
            collective_id=0, has_side_effects=True, vmem_limit_bytes=61 * 1024 * 1024
        ),
    )(
        leaf_inverse[0, 0],
        interior_rhs[0, 0],
        interface_rhs[0, 0],
        project_basis.reshape(leaves, blocks * rank, ls),
        lift_basis.reshape(leaves, blocks * rank, ls),
        cluster_basis[0, 0],
        interface_inverse[0],
        coarse_basis[0],
        coarse_inverse,
        couplings,
        ranks,
        owners,
    )
    interior, own = pl.pallas_call(
        finish,
        out_shape=(
            jax.ShapeDtypeStruct((leaves, ls, ports), F32),
            jax.ShapeDtypeStruct((cs, ports), F32),
        ),
        in_specs=[vmem] * 4 + [smem] * 2,
        out_specs=(hbm, hbm),
        scratch_shapes=[pltpu.VMEM((leaves, ls, ports), F32), dma((leaves,)), dma],
        compiler_params=pltpu.CompilerParams(vmem_limit_bytes=16 * 1024 * 1024),
    )(*held, couplings, ranks)
    return interior[None, None], own[None, None]


def shards(
    leaf_inverse,
    interior_rhs,
    interface_rhs,
    project_basis,
    lift_basis,
    cluster_basis,
    interface_inverse,
    coarse_basis,
    coarse_inverse,
    couplings,
    ranks,
    owners,
):
    linv_local = leaf_inverse[0, 0]
    leaves = couplings.shape[2]
    blocks = couplings.shape[3]
    rank_pad = project_basis.shape[4]
    port_count = interior_rhs.shape[4]
    cluster_width = cluster_basis.shape[3]
    sub_count = lax.axis_size("sub")
    block_count = leaves * blocks
    solved = jnp.einsum("lij,ljp->lip", linv_local, interior_rhs[0, 0], precision=highest)
    rank_mask = (
        jnp.arange(rank_pad, dtype=jnp.int32)[None, None, :] < ranks[0, 0][..., None]
    ).astype(jnp.float32)
    coefficients = (
        jnp.einsum("ljri,lip->ljrp", project_basis[0, 0], solved, precision=highest)
        * rank_mask[..., None]
    )
    flat_coef = coefficients.reshape(block_count, rank_pad, port_count)
    owner_table = owners[0]
    sub_range = jnp.arange(sub_count, dtype=jnp.int32)
    cluster_hot = (couplings[0, 0].reshape(block_count)[:, None] == sub_range[None, :]).astype(
        jnp.int32
    )
    target = jnp.sum(cluster_hot * owner_table[None, :], axis=1)
    owner_matrix = (owner_table[:, None] == sub_range[None, :]).astype(jnp.float32)
    capacity = max(2, block_count // sub_count)
    block_range = jnp.arange(block_count, dtype=jnp.int32)
    earlier = (target[:, None] == target[None, :]) & (block_range[None, :] < block_range[:, None])
    slot_index = jnp.sum(earlier.astype(jnp.int32), axis=1)
    slot_place = target * capacity + slot_index
    dispatch = (
        slot_place[:, None] == jnp.arange(sub_count * capacity, dtype=jnp.int32)[None, :]
    ).astype(jnp.float32)
    outgoing = jnp.einsum("mq,mrp->qrp", dispatch, flat_coef, precision=highest).reshape(
        sub_count, capacity, rank_pad, port_count
    )
    filled = jnp.sum(dispatch, axis=0).reshape(sub_count, capacity)
    incoming, filled_in = (
        lax.all_to_all(outgoing, "sub", split_axis=0, concat_axis=0, tiled=True),
        lax.all_to_all(filled, "sub", split_axis=0, concat_axis=0, tiled=True),
    )
    gathered_coef = jnp.sum(incoming, axis=(0, 1))
    own_basis = cluster_basis[0, 0]
    interface_terms = interface_rhs[0, 0] - lax.dot_general(
        own_basis, gathered_coef, (((0,), (0,)), ((), ())), precision=highest
    )
    port_share = port_count // sub_count
    by_share = interface_terms.T.reshape(sub_count, port_share * cluster_width)
    spread = lax.all_to_all(by_share, "sub", split_axis=0, concat_axis=0, tiled=True).reshape(
        sub_count, port_share, cluster_width
    )
    ordered = jnp.einsum("ks,spc->pkc", owner_matrix, spread, precision=highest).reshape(
        port_share, sub_count * cluster_width
    )
    local_part = lax.dot_general(
        ordered, interface_inverse[0], (((1,), (1,)), ((), ())), precision=highest
    )
    coarse_local = jnp.dot(ordered, coarse_basis[0], precision=highest)
    coarse_residual = lax.psum(coarse_local, "grp")
    coarse_solution = lax.dot_general(
        coarse_residual, coarse_inverse, (((1,), (1,)), ((), ())), precision=highest
    )
    solution = local_part + lax.dot_general(
        coarse_solution, coarse_basis[0], (((1,), (1,)), ((), ())), precision=highest
    )
    owner_order = jnp.einsum(
        "ks,pkc->spc",
        owner_matrix,
        solution.reshape(port_share, sub_count, cluster_width),
        precision=highest,
    )
    back_rows = lax.all_to_all(
        owner_order.reshape(sub_count, port_share * cluster_width),
        "sub",
        split_axis=0,
        concat_axis=0,
        tiled=True,
    )
    own_solution = back_rows.reshape(port_count, cluster_width).T
    lifted = jnp.dot(own_basis, own_solution, precision=highest)
    replies = filled_in[:, :, None, None] * lifted[None, None]
    returned = lax.all_to_all(replies, "sub", split_axis=0, concat_axis=0, tiled=True).reshape(
        -1, rank_pad, port_count
    )
    per_block = jnp.einsum("mq,qrp->mrp", dispatch, returned, precision=highest)
    per_block = per_block.reshape(leaves, blocks, rank_pad, port_count) * rank_mask[..., None]
    correction = jnp.einsum("ljri,ljrp->lip", lift_basis[0, 0], per_block, precision=highest)
    interior = solved - jnp.einsum("lij,ljp->lip", linv_local, correction, precision=highest)
    return (interior[None, None], own_solution[None, None])


def solution(mesh):
    in_specs = (
        P("sub", "grp", None, None, None),
        P("sub", "grp", None, None, None),
        P("sub", "grp", None, None),
        P("sub", "grp", None, None, None, None),
        P("sub", "grp", None, None, None, None),
        P("sub", "grp", None, None),
        P("grp", None, None),
        P("grp", None, None),
        P(),
        P("sub", "grp", None, None),
        P("sub", "grp", None, None),
        P("grp", None),
    )
    out_specs = (P("sub", "grp", None, None, None), P("sub", "grp", None, None))
    body = fused if mesh.shape["sub"] <= 8 else shards
    return jax.shard_map(body, mesh=mesh, in_specs=in_specs, out_specs=out_specs, check_vma=False)
```

```python
import functools

import jax
import jax.numpy as jnp
from jax import lax
from jax.experimental import pallas as pl
from jax.experimental.pallas import tpu as pltpu
from jax.sharding import PartitionSpec as P

highest = lax.Precision.HIGHEST
MESH = pl.DeviceIdType.MESH
F32 = jnp.float32
BF16 = jnp.bfloat16


def split(x):
    high = x.astype(BF16)
    return high, (x - high.astype(F32)).astype(BF16)


def dot(a, b, dims=((1,), (0,))):
    return lax.dot_general(a, b, (dims, ((), ())), preferred_element_type=F32)


def product(a, b, dims=((1,), (0,))):
    return dot(a[0], b[0], dims) + dot(a[0], b[1], dims) + dot(a[1], b[0], dims)


def narrow(a, b):
    width = b[0].shape[1]
    both = dot(a[0], jnp.concatenate([b[0], b[1]], axis=1))
    return both[:, :width] + both[:, width:] + dot(a[1], b[0])


def kernel(
    n,
    groups,
    linv_hbm,
    rhs_hbm,
    irhs_hbm,
    proj_hbm,
    lift_hbm,
    basis_hbm,
    inverse_hbm,
    coarse_hbm,
    cinv_hbm,
    couplings,
    ranks,
    owners,
    solved,
    back,
    lifted,
    own_out,
    linv,
    rhs,
    proj,
    lift,
    inverse,
    coarse,
    cinv,
    basis_own,
    irhs_own,
    pre_out,
    pre_in,
    sums,
    a_out,
    a_in,
    mid,
    mid_in,
    share,
    lift_all,
    sol,
    own_stage,
    own_in,
    gain,
    base,
    leaf_sem,
    misc_sem,
    pre_send,
    pre_recv,
    a_send,
    a_recv,
    m_send,
    m_recv,
    b_send,
    b_recv,
    o_send,
    o_recv,
):
    leaves, ls, ports = rhs.shape
    blocks = couplings.shape[2]
    rank, cs = basis_own.shape
    nco = coarse.shape[1]
    part = ports // n
    half_rank, half_part = rank // 2, part // 2
    me = lax.axis_index("sub")
    my_group = lax.axis_index("grp")

    def leaf_copy(l, which):
        pair = ((linv_hbm, linv), (rhs_hbm, rhs), (proj_hbm, proj), (lift_hbm, lift))[which]
        return pltpu.make_async_copy(pair[0].at[l], pair[1].at[l], leaf_sem.at[which, l])

    barrier = pltpu.get_barrier_semaphore()
    for d in range(1, n):
        pl.semaphore_signal(barrier, inc=1, device_id=(lax.rem(me + d, n), my_group), device_id_type=MESH)
    for d in range(1, groups):
        pl.semaphore_signal(barrier, inc=1, device_id=(me, lax.rem(my_group + d, groups)), device_id_type=MESH)
    for l in range(leaves):
        for which in range(3):
            leaf_copy(l, which).start()
    misc = (
        pltpu.make_async_copy(basis_hbm, basis_own, misc_sem.at[0]),
        pltpu.make_async_copy(irhs_hbm, irhs_own, misc_sem.at[1]),
        pltpu.make_async_copy(coarse_hbm, coarse, misc_sem.at[2]),
        pltpu.make_async_copy(inverse_hbm, inverse, misc_sem.at[3]),
        pltpu.make_async_copy(cinv_hbm, cinv, misc_sem.at[4]),
    )
    for copy in misc:
        copy.start()
    for l in range(leaves):
        leaf_copy(l, 3).start()

    sums[...] = jnp.zeros_like(sums)
    row_of = lax.broadcasted_iota(jnp.int32, (rank, ports), 0)

    def leaf_forward(l):
        for which in range(3):
            leaf_copy(l, which).wait()
        both = product(split(proj[l]), split(linv[l]))
        coef = narrow(split(both), split(rhs[l]))
        for j in range(blocks):
            kept = jnp.where(row_of < ranks[0, 0, j, l], coef[j * rank : (j + 1) * rank], 0.0)
            for k in range(n):
                sums[k] += jnp.where(couplings[0, 0, j, l] == k, kept, 0.0)

    misc[0].wait()
    misc[1].wait()
    packed = jnp.concatenate([basis_own[:half_rank], basis_own[half_rank:]], axis=1)
    irhs_t = irhs_own[...].T
    for t in range(n):
        pre_out[t, :half_rank] = packed
        rows = irhs_t[t * part : (t + 1) * part]
        pre_out[t, half_rank:] = jnp.concatenate([rows[:half_part], rows[half_part:]], axis=1)

    def peer(d):
        return (lax.rem(me + d, n), my_group)

    def source(d):
        return lax.rem(me - d + n, n)

    def remote(src, dst, send, recv, target):
        return pltpu.make_async_remote_copy(
            src_ref=src, dst_ref=dst, send_sem=send, recv_sem=recv, device_id=target, device_id_type=MESH
        )

    def pre_copy(d, slot):
        return remote(pre_out.at[lax.rem(me + d, n)], pre_in.at[slot], pre_send.at[d], pre_recv.at[d], peer(d))

    def sums_copy(d):
        return remote(a_out.at[lax.rem(me + d, n)], a_in.at[d], a_send.at[d], a_recv.at[d], peer(d))

    def mid_copy(d):
        target = (me, lax.rem(my_group + d, groups))
        return remote(mid, mid_in.at[d], m_send.at[d], m_recv.at[d], target)

    def gather_copy(d, slot):
        return remote(share, lift_all.at[slot], b_send.at[d], b_recv.at[d], peer(d))

    def own_copy(d, slot):
        return remote(own_stage.at[lax.rem(me + d, n)], own_in.at[slot], o_send.at[d], o_recv.at[d], peer(d))

    early = leaves * 2 // 8
    pl.loop(0, early)(leaf_forward)

    pl.semaphore_wait(barrier, n - 1 + groups - 1)
    for d in range(1, n):
        pre_copy(d, me).start()
    pre_in[me] = pre_out[me]

    pl.loop(early, leaves)(leaf_forward)

    sums_t = sums[...].reshape(n * rank, ports).T
    a_out[...] = sums_t.reshape(n, part, n * rank)
    for d in range(1, n):
        sums_copy(d).start()

    for copy in misc[2:]:
        copy.wait()
    for d in range(1, n):
        pre_copy(d, source(d)).wait_recv()
    got = [pre_in[owners[0, k]] for k in range(n)]
    stacked = jnp.concatenate(
        [half for g in got for half in (g[:half_rank, :cs], g[:half_rank, cs:])], axis=0
    )
    wide = jnp.concatenate([stacked] * n, axis=1)
    diag_row = lax.broadcasted_iota(jnp.int32, wide.shape, 0) // rank
    diag_col = lax.broadcasted_iota(jnp.int32, wide.shape, 1) // cs
    diagonal = split(jnp.where(diag_row == diag_col, wide, 0.0))
    irhs_share = jnp.concatenate(
        [jnp.concatenate([g[half_rank:, :cs], g[half_rank:, cs:]], axis=0) for g in got], axis=1
    )
    irhs_pair = split(irhs_share)
    coarse_pair = split(coarse[...])
    inverse_pair = split(inverse[...])
    basis_coarse = narrow(diagonal, coarse_pair)
    basis_coarse_pair = split(basis_coarse)
    left_pair = split(product(diagonal, inverse_pair))
    base[...] = product(irhs_pair, left_pair, ((1,), (1,)))
    gain[:, : n * rank] = -product(left_pair, diagonal, ((1,), (1,)))
    gain[:, n * rank :] = narrow(basis_coarse_pair, split(cinv[...]))
    coarse_base = narrow(irhs_pair, coarse_pair)

    total = a_out[me]
    for d in range(1, n):
        sums_copy(d).wait_recv()
        total = total + a_in[d]
    total_pair = split(total)
    residual = coarse_base - narrow(total_pair, basis_coarse_pair)
    mid[...] = residual
    for d in range(1, groups):
        mid_copy(d).start()

    def leaf_middle(l):
        leaf_copy(l, 3).wait()
        inv = split(linv[l])
        solved[l] = narrow(inv, split(rhs[l]))
        spread = product(inv, split(lift[l]), ((1,), (1,)))
        back[l] = jnp.concatenate(split(spread), axis=1)

    half = leaves // 4
    pl.loop(0, half)(leaf_middle)

    for d in range(1, groups):
        mid_copy(d).wait_recv()
        residual = residual + mid_in[d]
    known = jnp.concatenate([total, residual], axis=1)
    share[...] = base[...] + product(split(known), split(gain[...]), ((1,), (1,)))
    for d in range(1, n):
        gather_copy(d, me).start()
    lift_all[me] = share[...]

    by_cluster = split(irhs_share - product(total_pair, diagonal))
    coarse_solution = split(product(split(residual), split(cinv[...]), ((1,), (1,))))
    solution_t = product(by_cluster, inverse_pair, ((1,), (1,))) + product(coarse_solution, coarse_pair, ((1,), (1,)))
    for k in range(n):
        rows = solution_t[:, k * cs : (k + 1) * cs]
        sol[k] = jnp.concatenate([rows[:half_part], rows[half_part:]], axis=1)
    for t in range(n):
        place = jnp.int32(0)
        for k in range(n):
            place = jnp.where(owners[0, k] == t, k, place)
        own_stage[t] = sol[place]
    for d in range(1, n):
        own_copy(d, me).start()
    own_in[me] = own_stage[me]

    pl.loop(half, leaves)(leaf_middle)

    for d in range(1, n):
        gather_copy(d, source(d)).wait_recv()
    lifted[...] = lift_all[...].reshape(ports, n * rank).T.reshape(n, rank, ports)
    for d in range(1, n):
        own_copy(d, source(d)).wait_recv()
    rows = []
    for t in range(n):
        rows += [own_in[t][:, :cs], own_in[t][:, cs:]]
    own_out[...] = jnp.concatenate(rows, axis=0).T

    for d in range(1, n):
        pre_copy(d, me).wait_send()
        sums_copy(d).wait_send()
        gather_copy(d, me).wait_send()
        own_copy(d, me).wait_send()
    for d in range(1, groups):
        mid_copy(d).wait_send()


def finish(solved, back, lifted, own, couplings, ranks, interior_hbm, own_hbm, result, out_sem, own_sem):
    leaves, ls, ports = solved.shape
    blocks = couplings.shape[2]
    rank = lifted.shape[1]
    row_of = lax.broadcasted_iota(jnp.int32, (rank, ports), 0)
    own_copy = pltpu.make_async_copy(own, own_hbm, own_sem)
    own_copy.start()

    def out_copy(l):
        return pltpu.make_async_copy(result.at[l], interior_hbm.at[l], out_sem.at[l])

    for l in range(leaves):
        rows = []
        for j in range(blocks):
            rows.append(jnp.where(row_of < ranks[0, 0, j, l], lifted[couplings[0, 0, j, l]], 0.0))
        pair = jnp.concatenate(split(jnp.concatenate(rows, axis=0)), axis=1)
        both = dot(back[l], jnp.concatenate([pair, pair], axis=0))
        result[l] = solved[l] - (both[:, :ports] + both[:, ports:])
        out_copy(l).start()
    for l in range(leaves):
        out_copy(l).wait()
    own_copy.wait()


def fused(
    leaf_inverse,
    interior_rhs,
    interface_rhs,
    project_basis,
    lift_basis,
    cluster_basis,
    interface_inverse,
    coarse_basis,
    coarse_inverse,
    couplings,
    ranks,
    owners,
):
    n = lax.axis_size("sub")
    groups = lax.axis_size("grp")
    leaves, ls = leaf_inverse.shape[2:4]
    ports = interior_rhs.shape[4]
    blocks, rank = project_basis.shape[3:5]
    cs = cluster_basis.shape[3]
    nig = interface_inverse.shape[1]
    nco = coarse_basis.shape[2]
    part = ports // n
    hbm = pl.BlockSpec(memory_space=pltpu.HBM)
    smem = pl.BlockSpec(memory_space=pltpu.SMEM)
    vmem = pl.BlockSpec(memory_space=pltpu.VMEM)
    dma = pltpu.SemaphoreType.DMA
    couplings = jnp.swapaxes(couplings, 2, 3)
    ranks = jnp.swapaxes(ranks, 2, 3)
    held = pl.pallas_call(
        functools.partial(kernel, n, groups),
        out_shape=(
            pltpu.VMEM((leaves, ls, ports), F32),
            pltpu.VMEM((leaves, ls, 2 * blocks * rank), BF16),
            pltpu.VMEM((n, rank, ports), F32),
            pltpu.VMEM((cs, ports), F32),
        ),
        in_specs=[hbm] * 9 + [smem] * 3,
        out_specs=(vmem,) * 4,
        scratch_shapes=[
            pltpu.VMEM((leaves, ls, ls), F32),
            pltpu.VMEM((leaves, ls, ports), F32),
            pltpu.VMEM((leaves, blocks * rank, ls), F32),
            pltpu.VMEM((leaves, blocks * rank, ls), F32),
            pltpu.VMEM((nig, nig), F32),
            pltpu.VMEM((nig, nco), F32),
            pltpu.VMEM((nco, nco), F32),
            pltpu.VMEM((rank, cs), F32),
            pltpu.VMEM((cs, ports), F32),
            pltpu.VMEM((n, rank // 2 + part // 2, 2 * cs), F32),
            pltpu.VMEM((n, rank // 2 + part // 2, 2 * cs), F32),
            pltpu.VMEM((n, rank, ports), F32),
            pltpu.VMEM((n, part, n * rank), F32),
            pltpu.VMEM((n, part, n * rank), F32),
            pltpu.VMEM((part, nco), F32),
            pltpu.VMEM((groups, part, nco), F32),
            pltpu.VMEM((part, n * rank), F32),
            pltpu.VMEM((n, part, n * rank), F32),
            pltpu.VMEM((n, part // 2, 2 * cs), F32),
            pltpu.VMEM((n, part // 2, 2 * cs), F32),
            pltpu.VMEM((n, part // 2, 2 * cs), F32),
            pltpu.VMEM((n * rank, n * rank + nco), F32),
            pltpu.VMEM((part, n * rank), F32),
            dma((4, leaves)),
            dma((5,)),
        ]
        + [dma((n,))] * 4
        + [dma((groups,))] * 2
        + [dma((n,))] * 4,
        compiler_params=pltpu.CompilerParams(
            collective_id=0, has_side_effects=True, vmem_limit_bytes=61 * 1024 * 1024
        ),
    )(
        leaf_inverse[0, 0],
        interior_rhs[0, 0],
        interface_rhs[0, 0],
        project_basis.reshape(leaves, blocks * rank, ls),
        lift_basis.reshape(leaves, blocks * rank, ls),
        cluster_basis[0, 0],
        interface_inverse[0],
        coarse_basis[0],
        coarse_inverse,
        couplings,
        ranks,
        owners,
    )
    interior, own = pl.pallas_call(
        finish,
        out_shape=(
            jax.ShapeDtypeStruct((leaves, ls, ports), F32),
            jax.ShapeDtypeStruct((cs, ports), F32),
        ),
        in_specs=[vmem] * 4 + [smem] * 2,
        out_specs=(hbm, hbm),
        scratch_shapes=[pltpu.VMEM((leaves, ls, ports), F32), dma((leaves,)), dma],
        compiler_params=pltpu.CompilerParams(vmem_limit_bytes=16 * 1024 * 1024),
    )(*held, couplings, ranks)
    return interior[None, None], own[None, None]


def shards(
    leaf_inverse,
    interior_rhs,
    interface_rhs,
    project_basis,
    lift_basis,
    cluster_basis,
    interface_inverse,
    coarse_basis,
    coarse_inverse,
    couplings,
    ranks,
    owners,
):
    linv_local = leaf_inverse[0, 0]
    leaves = couplings.shape[2]
    blocks = couplings.shape[3]
    rank_pad = project_basis.shape[4]
    port_count = interior_rhs.shape[4]
    cluster_width = cluster_basis.shape[3]
    sub_count = lax.axis_size("sub")
    block_count = leaves * blocks
    solved = jnp.einsum("lij,ljp->lip", linv_local, interior_rhs[0, 0], precision=highest)
    rank_mask = (
        jnp.arange(rank_pad, dtype=jnp.int32)[None, None, :] < ranks[0, 0][..., None]
    ).astype(jnp.float32)
    coefficients = (
        jnp.einsum("ljri,lip->ljrp", project_basis[0, 0], solved, precision=highest)
        * rank_mask[..., None]
    )
    flat_coef = coefficients.reshape(block_count, rank_pad, port_count)
    owner_table = owners[0]
    sub_range = jnp.arange(sub_count, dtype=jnp.int32)
    cluster_hot = (couplings[0, 0].reshape(block_count)[:, None] == sub_range[None, :]).astype(
        jnp.int32
    )
    target = jnp.sum(cluster_hot * owner_table[None, :], axis=1)
    owner_matrix = (owner_table[:, None] == sub_range[None, :]).astype(jnp.float32)
    capacity = max(2, block_count // sub_count)
    block_range = jnp.arange(block_count, dtype=jnp.int32)
    earlier = (target[:, None] == target[None, :]) & (block_range[None, :] < block_range[:, None])
    slot_index = jnp.sum(earlier.astype(jnp.int32), axis=1)
    slot_place = target * capacity + slot_index
    dispatch = (
        slot_place[:, None] == jnp.arange(sub_count * capacity, dtype=jnp.int32)[None, :]
    ).astype(jnp.float32)
    outgoing = jnp.einsum("mq,mrp->qrp", dispatch, flat_coef, precision=highest).reshape(
        sub_count, capacity, rank_pad, port_count
    )
    filled = jnp.sum(dispatch, axis=0).reshape(sub_count, capacity)
    incoming, filled_in = (
        lax.all_to_all(outgoing, "sub", split_axis=0, concat_axis=0, tiled=True),
        lax.all_to_all(filled, "sub", split_axis=0, concat_axis=0, tiled=True),
    )
    gathered_coef = jnp.sum(incoming, axis=(0, 1))
    own_basis = cluster_basis[0, 0]
    interface_terms = interface_rhs[0, 0] - lax.dot_general(
        own_basis, gathered_coef, (((0,), (0,)), ((), ())), precision=highest
    )
    port_share = port_count // sub_count
    by_share = interface_terms.T.reshape(sub_count, port_share * cluster_width)
    spread = lax.all_to_all(by_share, "sub", split_axis=0, concat_axis=0, tiled=True).reshape(
        sub_count, port_share, cluster_width
    )
    ordered = jnp.einsum("ks,spc->pkc", owner_matrix, spread, precision=highest).reshape(
        port_share, sub_count * cluster_width
    )
    local_part = lax.dot_general(
        ordered, interface_inverse[0], (((1,), (1,)), ((), ())), precision=highest
    )
    coarse_local = jnp.dot(ordered, coarse_basis[0], precision=highest)
    coarse_residual = lax.psum(coarse_local, "grp")
    coarse_solution = lax.dot_general(
        coarse_residual, coarse_inverse, (((1,), (1,)), ((), ())), precision=highest
    )
    solution = local_part + lax.dot_general(
        coarse_solution, coarse_basis[0], (((1,), (1,)), ((), ())), precision=highest
    )
    owner_order = jnp.einsum(
        "ks,pkc->spc",
        owner_matrix,
        solution.reshape(port_share, sub_count, cluster_width),
        precision=highest,
    )
    back_rows = lax.all_to_all(
        owner_order.reshape(sub_count, port_share * cluster_width),
        "sub",
        split_axis=0,
        concat_axis=0,
        tiled=True,
    )
    own_solution = back_rows.reshape(port_count, cluster_width).T
    lifted = jnp.dot(own_basis, own_solution, precision=highest)
    replies = filled_in[:, :, None, None] * lifted[None, None]
    returned = lax.all_to_all(replies, "sub", split_axis=0, concat_axis=0, tiled=True).reshape(
        -1, rank_pad, port_count
    )
    per_block = jnp.einsum("mq,qrp->mrp", dispatch, returned, precision=highest)
    per_block = per_block.reshape(leaves, blocks, rank_pad, port_count) * rank_mask[..., None]
    correction = jnp.einsum("ljri,ljrp->lip", lift_basis[0, 0], per_block, precision=highest)
    interior = solved - jnp.einsum("lij,ljp->lip", linv_local, correction, precision=highest)
    return (interior[None, None], own_solution[None, None])


def solution(mesh):
    in_specs = (
        P("sub", "grp", None, None, None),
        P("sub", "grp", None, None, None),
        P("sub", "grp", None, None),
        P("sub", "grp", None, None, None, None),
        P("sub", "grp", None, None, None, None),
        P("sub", "grp", None, None),
        P("grp", None, None),
        P("grp", None, None),
        P(),
        P("sub", "grp", None, None),
        P("sub", "grp", None, None),
        P("grp", None),
    )
    out_specs = (P("sub", "grp", None, None, None), P("sub", "grp", None, None))
    body = fused if mesh.shape["sub"] <= 8 else shards
    return jax.shard_map(body, mesh=mesh, in_specs=in_specs, out_specs=out_specs, check_vma=False)
```
